256 devices in a mesh: row: 64 (over x, z, core), col: 4 (over y).
Axes of the slice: x: 4, y: 4, z: 8, core: 2. Of those that a mesh axis runs over, the one named last changes fastest.
Arguments:
- matrix: float32 [16384, 16384], P('row', 'col'), as said below
Outputs:
- factored: float32 [16384, 16384], P('row', 'col')
Inputs may be any that keep to these rules, and one draw needn't show every extreme that they name: matrix read in matrix order is symmetric except in its first tile column below the first tile, which holds the panel's factor with entries of order 0.1; diagonal entries lie between 24 and 40, and the tile of updated at rows and columns 128 to 255 is positive definite.
All inputs are finite; a program needn't handle non-finite values.
Results may differ from the reference program's by a relative error of at most 0.00005.
Values sent between devices are 32-bit elements; how exact they have to be, the bound alone decides.
No kernel may reach another device: no remote copies, remote signals or barrier semaphores. Data moves between devices by JAX's collectives and lax.ppermute only.
A program may use at most 64 MiB of HBM per device.

```python
import math
import jax
import jax.numpy as jnp
from jax import lax

NB = 128
TR = 2
ORDER = 16384
TC = 32
N_ROW = 64
N_COL = 4


def draw_matrix(key, part):
    key = jax.random.fold_in(key, 7)
    first, second, third = jax.random.split(key, 3)
    noise = jnp.clip(jax.random.normal(first, (ORDER, ORDER), jnp.float32), -4.0, 4.0)
    factor_part = jnp.clip(jax.random.normal(third, (ORDER, NB), jnp.float32), -4.0, 4.0)
    symmetric = (noise + noise.T) * (0.6 / math.sqrt(2.0))
    diagonal = jax.random.uniform(second, (ORDER,), jnp.float32, 24.0, 39.8)
    indices = jnp.arange(ORDER)
    dense = jnp.where(indices[:, None] == indices[None, :], diagonal[:, None], symmetric)
    dense = dense.at[NB:2 * NB, NB:2 * NB].add(jnp.float32(0.2))
    dense = dense.at[NB:, :NB].set(0.1 * factor_part[NB:])
    return dense.reshape(TR, N_ROW, NB, TC, N_COL, NB).transpose(1, 0, 2, 4, 3, 5).reshape(ORDER, ORDER)


def setup_inputs(seed: int = 0) -> dict:
    key_of = jax.random.split(jax.random.key(seed), 2)
    return {
        "matrix": draw_matrix(jax.random.fold_in(key_of[1], 71), 0),
    }


def to_matrix(stored):
    return stored.reshape(N_ROW, TR, NB, N_COL, TC, NB).transpose(1, 0, 2, 4, 3, 5).reshape(ORDER, ORDER)

def to_storage(dense):
    return dense.reshape(TR, N_ROW, NB, TC, N_COL, NB).transpose(1, 0, 2, 4, 3, 5).reshape(ORDER, ORDER)

def reference(matrix):
    dense = to_matrix(matrix)
    row_ids = jnp.arange(ORDER, dtype=jnp.int32)
    panel = jnp.where((row_ids >= NB)[:, None], dense[:, :NB], jnp.float32(0.0))
    product = jnp.dot(panel.astype(jnp.float32), panel.T.astype(jnp.float32), precision=lax.Precision.HIGHEST, preferred_element_type=jnp.float32)
    updated = dense - product
    pivot = updated[NB:2 * NB, NB:2 * NB]
    lower = jnp.linalg.cholesky(pivot)
    column = updated[:, NB:2 * NB]
    solved = jax.scipy.linalg.solve_triangular(lower, column.T, lower=True).T
    tile_ids = row_ids // NB
    stacked = jnp.tile(lower, (ORDER // NB, 1))
    fresh = jnp.where((tile_ids >= 2)[:, None], solved, jnp.where((tile_ids == 1)[:, None], stacked, column))
    result = jnp.concatenate([updated[:, :NB], fresh, updated[:, 2 * NB:]], axis=1)
    return to_storage(result)
```

```python
import jax
import jax.numpy as jnp
from jax import lax
from jax.experimental import pallas as pl
from jax.experimental.pallas import tpu as pltpu
from jax.sharding import PartitionSpec as P

NB = 128
NX, NY, NZ, NC = 4, 4, 8, 2
AXES = ("row", "col")
HIGH = lax.Precision.HIGHEST
TRANS = (((1,), (1,)), ((), ()))


def rank(x, y, z, c):
    return ((x * NZ + z) * NC + c) * NY + y


def chips(xs=range(NX), zs=range(NZ), cs=range(NC), ys=range(NY)):
    return [(x, y, z, c) for x in xs for z in zs for c in cs for y in ys]


def shift(block, move, **where):
    pairs = [(rank(*d), rank(*move(*d))) for d in chips(**where)]
    return lax.ppermute(block, AXES, pairs)


def split(v):
    hi = v.astype(jnp.bfloat16)
    lo = (v - hi.astype(jnp.float32)).astype(jnp.bfloat16)
    return hi, lo


def pivot_kernel(a_ref, p_ref, u_ref):
    p = p_ref[...]
    u_ref[...] = a_ref[...] - lax.dot_general(
        p, p, TRANS, precision=HIGH, preferred_element_type=jnp.float32
    )


def factor_kernel(u_ref, low_ref, inv_ref):
    blocks = NB // 8
    lane = lax.broadcasted_iota(jnp.int32, (8, NB), 1)
    sub = lax.broadcasted_iota(jnp.int32, (8, NB), 0)
    s = [u_ref[8 * i : 8 * i + 8, :] for i in range(blocks)]
    t = [(lane == sub + 8 * i).astype(jnp.float32) for i in range(blocks)]
    for j in range(NB):
        b, k = divmod(j, 8)
        row, row_t = s[b][k : k + 1, :], t[b][k : k + 1, :]
        scale = 1.0 / row[:, j : j + 1]
        row, row_t = row * scale, row_t * scale
        for i in range(b, blocks):
            col = jnp.broadcast_to(s[i][:, j : j + 1], (8, NB))
            if i == b:
                col = jnp.where(sub > k, col, 0.0)
            s[i] = s[i] - col * row
            t[i] = t[i] - col * row_t
    upper = []
    for i in range(blocks):
        diag = jnp.sum(jnp.where(lane == sub + 8 * i, s[i], 0.0), axis=1, keepdims=True)
        scale = 1.0 / jnp.sqrt(diag)
        upper.append(jnp.where(lane >= sub + 8 * i, s[i] * scale, 0.0))
        inv_ref[8 * i : 8 * i + 8, :] = t[i] * scale
    low_ref[...] = jnp.concatenate(upper, axis=0).T


def update_kernel(idx_ref, a_ref, p_ref, own_ref, got_ref, low_ref, inv_ref, out_ref, buf, sem):
    x, z, core, y = idx_ref[0], idx_ref[1], idx_ref[2], idx_ref[3]
    row0 = idx_ref[4]
    ph, plo = split(p_ref[...])

    def tile(step, _):
        src = step // 16
        piece = lax.rem(step, 16)
        dx, d = piece // 4, lax.rem(piece, 4)
        level = lax.rem(src + 1 + core, 2)
        m = level * 16 + lax.rem(x + dx, NX) * 4 + (d ^ lax.rem(z, 4))
        rows = pl.ds(pl.multiple_of(piece * NB, NB), NB)
        cols = pl.ds(pl.multiple_of(m * NB, NB), NB)

        def work(ref):
            qh, ql = split(ref[rows, :])
            prod = lax.dot_general(ph, qh, TRANS, preferred_element_type=jnp.float32)
            prod += lax.dot_general(ph, ql, TRANS, preferred_element_type=jnp.float32)
            prod += lax.dot_general(plo, qh, TRANS, preferred_element_type=jnp.float32)
            buf[:, cols] = a_ref[:, cols] - prod

        @pl.when(src == 0)
        def _():
            work(own_ref)

        @pl.when(src == 1)
        def _():
            work(got_ref)

        @pl.when((m == 0) & (y == 1))
        def _():
            column = buf[:, :NB]
            solved = lax.dot_general(
                column, inv_ref[...], TRANS, precision=HIGH, preferred_element_type=jnp.float32
            )
            top, bottom = column[:NB], solved[NB:]
            buf[NB:, :NB] = bottom
            keep = jnp.where(row0 == 1, low_ref[...], solved[:NB])
            buf[:NB, :NB] = jnp.where(row0 == 0, top, keep)

        pltpu.make_async_copy(buf.at[:, cols], out_ref.at[:, cols], sem).start()
        return 0

    lax.fori_loop(0, 32, tile, 0)
    pltpu.make_async_copy(buf, out_ref, sem).wait()


def vmem():
    return pl.BlockSpec(memory_space=pltpu.VMEM)


def smem():
    return pl.BlockSpec(memory_space=pltpu.SMEM)


def on_device(matrix):
    row = lax.axis_index("row")
    y = lax.axis_index("col")
    x, z, core = row // (NZ * NC), row // NC % NZ, row % NC
    tile = jax.ShapeDtypeStruct((NB, NB), jnp.float32)

    panel0 = matrix[:, :NB]
    panel0 = jnp.where((jnp.arange(2 * NB) >= NB)[:, None] | (row > 0), panel0, 0.0)

    first = lax.ppermute(panel0[:NB], AXES, [(rank(0, 0, 0, 1), rank(0, 1, 0, 1))])
    pivot = pl.pallas_call(
        pivot_kernel,
        out_shape=tile,
        grid=(1,),
        in_specs=[
            pl.BlockSpec((NB, NB), lambda i: (0, 0)),
            pl.BlockSpec((NB, NB), lambda i: (0, 0)),
        ],
        out_specs=pl.BlockSpec((NB, NB), lambda i: (0, 0)),
    )(matrix, first)

    piece = jnp.zeros((NB, NB), jnp.float32)
    for a in range(2):
        for c in range(2):
            got = shift(
                panel0[(1 - c) * NB : (2 - c) * NB],
                lambda X, Y, Z, C: (X, 2 * (Z % 2) + C, 4 * a + Z // 2, c),
                ys=[0],
            )
            piece = jnp.where((z // 4 == a) & (core == c), got, piece)

    panel = panel0
    for dy in (1, 3, 2):
        got = shift(panel0, lambda X, Y, Z, C: (X, dy, Z, C), ys=[0])
        panel = jnp.where(y == dy, got, panel)

    parts = [piece] + [
        shift(piece, lambda X, Y, Z, C: (X, Y, Z ^ d, C)) for d in (1, 2, 3)
    ]
    here = jnp.concatenate(parts)

    got = shift(pivot, lambda X, Y, Z, C: (0, 1, 7, 1), xs=[0], ys=[1], zs=[0], cs=[1])
    pivot = jnp.where(z == 7, got, pivot)
    best = pivot
    for d in (1, 2, 3):
        got = shift(pivot, lambda X, Y, Z, C: (X, Y, Z ^ d, C), xs=[0], ys=[1], zs=[0, 7], cs=[1])
        best = jnp.where((z == d) | (z == 7 ^ d), got, best)
    pivot = best
    for dx in (1, 3, 2):
        got = shift(pivot, lambda X, Y, Z, C: (dx, Y, Z, C), xs=[0], ys=[1], cs=[1])
        best = jnp.where(x == dx, got, best)
    pivot = best
    got = shift(pivot, lambda X, Y, Z, C: (X, Y, Z, 0), ys=[1], cs=[1])
    pivot = jnp.where(core == 0, got, pivot)

    left = shift(here, lambda X, Y, Z, C: ((X + 1) % NX, Y, Z, C))
    right = shift(here, lambda X, Y, Z, C: ((X + 3) % NX, Y, Z, C))
    far_a = shift(left[: 2 * NB], lambda X, Y, Z, C: ((X + 1) % NX, Y, Z, C))
    far_b = shift(right[2 * NB :], lambda X, Y, Z, C: ((X + 3) % NX, Y, Z, C))
    own = jnp.concatenate([here, right, far_a, far_b, left])

    other = shift(own, lambda X, Y, Z, C: (X, Y, Z, 1 - C))

    lower, inverse = pl.pallas_call(
        factor_kernel, out_shape=(tile, tile), in_specs=[vmem()], out_specs=(vmem(), vmem())
    )(pivot)

    index = jnp.stack([x, z, core, y, row]).astype(jnp.int32)
    return pl.pallas_call(
        update_kernel,
        out_shape=jax.ShapeDtypeStruct(matrix.shape, jnp.float32),
        in_specs=[smem()] + [vmem()] * 6,
        out_specs=pl.BlockSpec(memory_space=pl.ANY),
        scratch_shapes=[
            pltpu.VMEM(matrix.shape, jnp.float32),
            pltpu.SemaphoreType.DMA,
        ],
        compiler_params=pltpu.CompilerParams(vmem_limit_bytes=32 * 1024 * 1024),
    )(index, matrix, panel, own, other, lower, inverse)


def solution(mesh):
    return jax.shard_map(
        on_device,
        mesh=mesh,
        in_specs=(P("row", "col"),),
        out_specs=P("row", "col"),
        check_vma=False,
    )
```

```python
import jax
import jax.numpy as jnp
from jax import lax
from jax.experimental import pallas as pl
from jax.experimental.pallas import tpu as pltpu
from jax.sharding import PartitionSpec as P

NB = 128
NX, NY, NZ, NC = 4, 4, 8, 2
AXES = ("row", "col")
HIGH = lax.Precision.HIGHEST
TRANS = (((1,), (1,)), ((), ()))
MIB = 1024 * 1024


def rank(x, y, z, c):
    return ((x * NZ + z) * NC + c) * NY + y


def move(block, to, where=lambda x, y, z, c: True):
    pairs = [
        (rank(x, y, z, c), rank(*to(x, y, z, c)))
        for x in range(NX)
        for z in range(NZ)
        for c in range(NC)
        for y in range(NY)
        if where(x, y, z, c)
    ]
    return lax.ppermute(block, AXES, pairs)


def split(v):
    hi = v.astype(jnp.bfloat16)
    lo = (v - hi.astype(jnp.float32)).astype(jnp.bfloat16)
    return hi, lo


def times_transposed(left_hi, left_both, right):
    hi, lo = split(right)
    both = lax.dot_general(
        left_both, jnp.concatenate([hi, hi], axis=1), TRANS, preferred_element_type=jnp.float32
    )
    return both + lax.dot_general(left_hi, lo, TRANS, preferred_element_type=jnp.float32)


def factor_kernel(a_ref, p_ref, low_ref, inv_ref, u_ref):
    p = p_ref[...]
    u_ref[...] = a_ref[...] - lax.dot_general(
        p, p, TRANS, precision=HIGH, preferred_element_type=jnp.float32
    )
    n = NB // 8
    lane = lax.broadcasted_iota(jnp.int32, (8, NB), 1)
    sub = lax.broadcasted_iota(jnp.int32, (8, NB), 0)
    s = [u_ref[8 * i : 8 * i + 8, :] for i in range(n)]
    t = [(lane == sub + 8 * i).astype(jnp.float32) for i in range(n)]

    def spread(v, k):
        return jnp.broadcast_to(v[k : k + 1, :], (8, NB))

    for b in range(n):
        cols = [
            [jnp.broadcast_to(s[i][:, 8 * b + k : 8 * b + k + 1], (8, NB)) for i in range(b, n)]
            for k in range(8)
        ]
        factors = []
        for k in range(8):
            inv = 1.0 / spread(cols[k][0], k)
            f = [c * inv for c in cols[k]]
            f[0] = jnp.where(sub > k, f[0], 0.0)
            factors.append(f)
            for m in range(k + 1, 8):
                e = spread(cols[m][0], k)
                cols[m] = [c - g * e for c, g in zip(cols[m], f)]
            r, q = spread(s[b], k), spread(t[b], k)
            s[b] = s[b] - f[0] * r
            t[b] = t[b] - f[0] * q
        for k in range(8):
            r, q = spread(s[b], k), spread(t[b], k)
            for i in range(1, n - b):
                s[b + i] = s[b + i] - factors[k][i] * r
                t[b + i] = t[b + i] - factors[k][i] * q
    upper = []
    for i in range(n):
        diag = jnp.sum(jnp.where(lane == sub + 8 * i, s[i], 0.0), axis=1, keepdims=True)
        scale = 1.0 / jnp.sqrt(diag)
        upper.append(jnp.where(lane >= sub + 8 * i, s[i] * scale, 0.0))
        inv_ref[8 * i : 8 * i + 8, :] = t[i] * scale
    low_ref[...] = jnp.concatenate(upper, axis=0).T


def place():
    row = lax.axis_index("row")
    return row // (NZ * NC), row // NC % NZ, row % NC, lax.axis_index("col"), row


def panels(y, p_ref):
    p = jnp.where(y == 0, p_ref[0][...], jnp.where(y == 1, p_ref[1][...], p_ref[2][...]))
    hi, lo = split(p)
    return hi, jnp.concatenate([hi, lo], axis=1)


def update_kernel(hops, last, a_ref, *refs):
    p_refs, refs = refs[:3], refs[3:]
    count = 8 if last else 2 * len(hops)
    pieces, refs = refs[:count], refs[count:]
    if last:
        low_ref, inv_ref, refs = refs[0], refs[1], refs[2:]
    if hops[0] != 0:
        refs = refs[1:]
    out_ref, a_buf, o_buf, in_sem, out_sem = refs[:5]
    x, z, core, y, row = place()
    even = z % 2 == y // 2
    slots = [jnp.where(even ^ (d % 2 == 1), z ^ d, 7 - (z ^ d)) // 2 for d in (0, 2, 1, 3)]
    groups = [(e, s) for e in hops for s in range(2)]

    def start_of(e, s):
        level = lax.rem(s + 1 + core, 2)
        return (level * 4 + (x ^ e)) * 4 * NB

    ins = []
    for i, (e, s) in enumerate(groups):
        cols = pl.ds(pl.multiple_of(start_of(e, s), 4 * NB), 4 * NB)
        ins.append(pltpu.make_async_copy(a_ref.at[:, cols], a_buf.at[i], in_sem.at[i]))
        ins[-1].start()
    if last:
        col_buf, res_buf, piece_buf, col_sem, res_sem = refs[5:]
        col_in = pltpu.make_async_copy(a_ref.at[:, :NB], col_buf, col_sem)
        col_in.start()
    hi, both = panels(y, p_refs)

    special = y == 1
    if last:
        for e in range(4):
            for s in range(2):
                for d in range(4):

                    @pl.when((x == e) & (core == 1 - s) & (slots[d] == 0))
                    def _():
                        piece_buf[...] = pieces[2 * e + s][d * NB : (d + 1) * NB, :]

        col_in.wait()

        @pl.when(special)
        def _():
            column = col_buf[...] - times_transposed(hi, both, piece_buf[...])
            solved = lax.dot_general(
                column, inv_ref[...], TRANS, precision=HIGH, preferred_element_type=jnp.float32
            )
            res_buf[NB:, :] = solved[NB:]
            keep = jnp.where(row == 1, low_ref[...], solved[:NB])
            res_buf[:NB, :] = jnp.where(row == 0, column[:NB], keep)
            pltpu.make_async_copy(res_buf, out_ref.at[:, :NB], res_sem).start()

    outs = []
    for i, (e, s) in enumerate(groups):
        ref = pieces[2 * e + s] if last else pieces[i]
        prod = times_transposed(hi, both, ref[...])
        ins[i].wait()
        for d in range(4):
            cols = pl.ds(pl.multiple_of(slots[d] * NB, NB), NB)
            o_buf[i, :, cols] = a_buf[i, :, cols] - prod[:, d * NB : (d + 1) * NB]
        begin = start_of(e, s)
        for d in range(4):
            cols = pl.ds(pl.multiple_of(begin + d * NB, NB), NB)
            copy = pltpu.make_async_copy(
                o_buf.at[i, :, d * NB : (d + 1) * NB], out_ref.at[:, cols], out_sem.at[i, d]
            )
            write = jnp.logical_not(special & (begin + d * NB == 0)) if last else None
            outs.append((copy, write))
            if write is None:
                copy.start()
            else:
                pl.when(write)(copy.start)
    for copy, write in outs:
        if write is None:
            copy.wait()
        else:
            pl.when(write)(copy.wait)
    if last:

        @pl.when(special)
        def _():
            pltpu.make_async_copy(res_buf, out_ref.at[:, :NB], res_sem).wait()


def vmem():
    return pl.BlockSpec(memory_space=pltpu.VMEM)


def update(hops, matrix, cands, pieces, out=None, factors=()):
    last = len(factors) > 0
    groups = 2 * len(hops)
    hbm = pl.BlockSpec(memory_space=pltpu.HBM)
    args = [matrix, *cands, *pieces, *factors]
    specs = [hbm] + [vmem()] * (len(args) - 1)
    alias = {}
    if out is not None:
        alias = {len(args): 0}
        args.append(out)
        specs.append(hbm)
    scratch = [
        pltpu.VMEM((groups, 2 * NB, 4 * NB), jnp.float32),
        pltpu.VMEM((groups, 2 * NB, 4 * NB), jnp.float32),
        pltpu.SemaphoreType.DMA((groups,)),
        pltpu.SemaphoreType.DMA((groups, 4)),
    ]
    if last:
        scratch += [
            pltpu.VMEM((2 * NB, NB), jnp.float32),
            pltpu.VMEM((2 * NB, NB), jnp.float32),
            pltpu.VMEM((NB, NB), jnp.float32),
            pltpu.SemaphoreType.DMA,
            pltpu.SemaphoreType.DMA,
        ]

    def kernel(*refs):
        update_kernel(hops, last, *refs)

    return pl.pallas_call(
        kernel,
        out_shape=jax.ShapeDtypeStruct(matrix.shape, jnp.float32),
        in_specs=specs,
        out_specs=hbm,
        scratch_shapes=scratch,
        input_output_aliases=alias,
        compiler_params=pltpu.CompilerParams(vmem_limit_bytes=16 * MIB),
        cost_estimate=pl.CostEstimate(
            flops=groups * 2 * NB * NB * 4 * NB * 8,
            bytes_accessed=groups * 2 * NB * 4 * NB * 8,
            transcendentals=0,
        ),
    )(*args)


def on_device(matrix):
    x, z, core, y, row = place()
    tile = jax.ShapeDtypeStruct((NB, NB), jnp.float32)

    panel = matrix[:, :NB]
    panel = jnp.where((jnp.arange(2 * NB) >= NB)[:, None] | (row > 0), panel, 0.0)

    plane = lambda X, Y, Z, C: 2 * (Z % 2) + C
    source = lambda X, Y, Z, C: Y == 0
    got_a = move(panel[:NB], lambda X, Y, Z, C: (X, plane(X, Y, Z, C), Z, 1), source)
    got_b = move(panel[NB:], lambda X, Y, Z, C: (X, plane(X, Y, Z, C), Z, 0), source)
    piece = jnp.where(core == 1, got_a, got_b)

    rows_a = move(panel, lambda X, Y, Z, C: (X, Y ^ 1, Z, C))
    piece, rows_a = lax.optimization_barrier((piece, rows_a))
    rows_b = move(
        jnp.where(y == 1, rows_a, panel), lambda X, Y, Z, C: (X, Y ^ 3, Z, C)
    )

    tile_of = lambda X, Y, Z, C: Y < 2 and (X, Z, C) == (0, 0, 1)
    seed, piece = lax.optimization_barrier((panel[:NB], piece))
    got = move(seed, lambda X, Y, Z, C: (X, Y, 7, C), tile_of)
    seed = jnp.where(z == 7, got, seed)
    got = move(
        seed,
        lambda X, Y, Z, C: (X, Y, Z ^ 2, C),
        lambda X, Y, Z, C: Y < 2 and X == 0 and C == 1 and Z in (0, 7),
    )
    seed = jnp.where((z == 2) | (z == 5), got, seed)
    got = move(
        seed,
        lambda X, Y, Z, C: (X, Y, Z ^ 1, C),
        lambda X, Y, Z, C: Y < 2 and X == 0 and C == 1 and Z in (0, 2, 5, 7),
    )
    seed = jnp.where((z == 1) | (z == 3) | (z == 4) | (z == 6), got, seed)
    got = move(
        seed,
        lambda X, Y, Z, C: (2, Y, Z, C),
        lambda X, Y, Z, C: Y < 2 and X == 0 and C == 1,
    )
    seed = jnp.where(x == 2, got, seed)
    got = move(
        seed,
        lambda X, Y, Z, C: (X + 1, Y, Z, C),
        lambda X, Y, Z, C: Y < 2 and X in (0, 2) and C == 1,
    )
    seed = jnp.where((x == 1) | (x == 3), got, seed)
    got = move(seed, lambda X, Y, Z, C: (X, Y, Z, 0), lambda X, Y, Z, C: Y < 2 and C == 1)
    seed = jnp.where(core == 0, got, seed)
    pivot_rows = move(seed, lambda X, Y, Z, C: (X, 1, Z, C), lambda X, Y, Z, C: Y == 0)

    holds = lambda X, Y, Z, C: Z % 2 == Y // 2
    mirrored = move(piece, lambda X, Y, Z, C: (X, Y, 7 - Z, C), holds)
    piece = jnp.where(z % 2 == y // 2, piece, mirrored)

    two = jnp.concatenate([piece, move(piece, lambda X, Y, Z, C: (X, Y, Z ^ 2, C))])
    two, rows_b = lax.optimization_barrier((two, rows_b))
    cands = [panel, rows_a, rows_b]
    four = jnp.concatenate([two, move(two, lambda X, Y, Z, C: (X, Y, Z ^ 1, C))])

    factors = pl.pallas_call(
        factor_kernel,
        out_shape=(tile, tile),
        in_specs=[vmem(), vmem()],
        out_specs=(vmem(), vmem()),
        scratch_shapes=[pltpu.VMEM((NB, NB), jnp.float32)],
        compiler_params=pltpu.CompilerParams(vmem_limit_bytes=8 * MIB),
        cost_estimate=pl.CostEstimate(
            flops=6 * 10**9, bytes_accessed=3 * NB * NB * 4, transcendentals=0
        ),
    )(seed, pivot_rows)

    other = lambda X, Y, Z, C: (X, Y, Z, 1 - C)
    near_a = move(four, lambda X, Y, Z, C: (X ^ 1, Y, Z, C))
    near_b = move(four, lambda X, Y, Z, C: (X ^ 3, Y, Z, C))
    four_o = move(four, other)
    far = jnp.concatenate(
        [
            move(near_b[: 2 * NB], lambda X, Y, Z, C: (X ^ 1, Y, Z, C)),
            move(near_a[2 * NB :], lambda X, Y, Z, C: (X ^ 3, Y, Z, C)),
        ]
    )
    near_a_o, near_b_o = move(near_a, other), move(near_b, other)
    far, factors = lax.optimization_barrier((far, factors))
    far_o = move(far, other)

    out = update((0,), matrix, cands, [four, four_o])
    out = update((1, 3), matrix, cands, [near_a, near_a_o, near_b, near_b_o], out)
    pieces = [four, four_o, near_a, near_a_o, far, far_o, near_b, near_b_o]
    return update((2,), matrix, cands, pieces, out, factors)


def solution(mesh):
    return jax.shard_map(
        on_device,
        mesh=mesh,
        in_specs=(P("row", "col"),),
        out_specs=P("row", "col"),
        check_vma=False,
    )
```

```python
import jax
import jax.numpy as jnp
from jax import lax
from jax.experimental import pallas as pl
from jax.experimental.pallas import tpu as pltpu
from jax.sharding import PartitionSpec as P

NB = 128
HALF = NB // 2
NX, NY, NZ, NC = 4, 4, 8, 2
AXES = ("row", "col")
HIGH = lax.Precision.HIGHEST
TRANS = (((1,), (1,)), ((), ()))
MIB = 1024 * 1024


def rank(x, y, z, c):
    return ((x * NZ + z) * NC + c) * NY + y


def move(block, to, where=lambda x, y, z, c: True):
    pairs = [
        (rank(x, y, z, c), rank(*to(x, y, z, c)))
        for x in range(NX)
        for z in range(NZ)
        for c in range(NC)
        for y in range(NY)
        if where(x, y, z, c)
    ]
    return lax.ppermute(block, AXES, pairs)


def split(v):
    hi = v.astype(jnp.bfloat16)
    lo = (v - hi.astype(jnp.float32)).astype(jnp.bfloat16)
    return hi, lo


def times_transposed(left_hi, left_both, right):
    hi, lo = split(right)
    both = lax.dot_general(
        left_both, jnp.concatenate([hi, hi], axis=1), TRANS, preferred_element_type=jnp.float32
    )
    return both + lax.dot_general(left_hi, lo, TRANS, preferred_element_type=jnp.float32)


def place():
    row = lax.axis_index("row")
    return row // (NZ * NC), row // NC % NZ, row % NC, lax.axis_index("col"), row


def factor_kernel(a_ref, p_ref, low_ref, inv_ref, u_ref):
    x, z, core, y, row = place()
    here = (row == 1) & (y == 1)

    @pl.when(here)
    def _():
        factor(a_ref, p_ref, low_ref, inv_ref, u_ref)

    @pl.when(jnp.logical_not(here))
    def _():
        low_ref[...] = jnp.zeros((NB, NB), jnp.float32)
        inv_ref[...] = jnp.zeros((NB, NB), jnp.float32)


def factor(a_ref, p_ref, low_ref, inv_ref, u_ref):
    p = p_ref[...]
    u_ref[...] = a_ref[...] - lax.dot_general(
        p, p, TRANS, precision=HIGH, preferred_element_type=jnp.float32
    )
    n = NB // 8
    lane = lax.broadcasted_iota(jnp.int32, (8, NB), 1)
    sub = lax.broadcasted_iota(jnp.int32, (8, NB), 0)
    s = [u_ref[8 * i : 8 * i + 8, :] for i in range(n)]
    t = [(lane == sub + 8 * i).astype(jnp.float32) for i in range(n)]

    def spread(v, k):
        return jnp.broadcast_to(v[k : k + 1, :], (8, NB))

    for b in range(n):
        cols = [
            [jnp.broadcast_to(s[i][:, 8 * b + k : 8 * b + k + 1], (8, NB)) for i in range(b, n)]
            for k in range(8)
        ]
        factors = []
        for k in range(8):
            inv = 1.0 / spread(cols[k][0], k)
            f = [c * inv for c in cols[k]]
            f[0] = jnp.where(sub > k, f[0], 0.0)
            factors.append(f)
            for m in range(k + 1, 8):
                e = spread(cols[m][0], k)
                cols[m] = [c - g * e for c, g in zip(cols[m], f)]
            r, q = spread(s[b], k), spread(t[b], k)
            s[b] = s[b] - f[0] * r
            t[b] = t[b] - f[0] * q
        for k in range(8):
            r, q = spread(s[b], k), spread(t[b], k)
            for i in range(1, n - b):
                s[b + i] = s[b + i] - factors[k][i] * r
                t[b + i] = t[b + i] - factors[k][i] * q
    upper = []
    for i in range(n):
        diag = jnp.sum(jnp.where(lane == sub + 8 * i, s[i], 0.0), axis=1, keepdims=True)
        scale = 1.0 / jnp.sqrt(diag)
        upper.append(jnp.where(lane >= sub + 8 * i, s[i] * scale, 0.0))
        inv_ref[8 * i : 8 * i + 8, :] = t[i] * scale
    low_ref[...] = jnp.concatenate(upper, axis=0).T


def forward_kernel(panel_ref, rows_ref, out_ref):
    x, z, core, y, row = place()
    out_ref[...] = jnp.where(y == 1, rows_ref[...], panel_ref[...])


def panels(y, p_ref):
    p = jnp.where(y == 0, p_ref[0][...], jnp.where(y == 1, p_ref[1][...], p_ref[2][...]))
    hi, lo = split(p)
    return hi, jnp.concatenate([hi, lo], axis=1)


def update_kernel(hops, last, a_ref, *refs):
    p_refs, refs = refs[:3], refs[3:]
    count = 8 if last else 2 * len(hops)
    pieces, refs = refs[:count], refs[count:]
    if last:
        low_ref, inv_ref, refs = refs[0], refs[1], refs[2:]
    if hops[0] != 0:
        refs = refs[1:]
    out_ref, a_buf, o_buf, in_sem, out_sem = refs[:5]
    x, z, core, y, row = place()
    even = z % 2 == y // 2
    slots = [jnp.where(even ^ (d % 2 == 1), z ^ d, 7 - (z ^ d)) // 2 for d in (0, 2, 1, 3)]
    groups = [(e, s) for e in hops for s in range(2)]

    def start_of(e, s):
        level = lax.rem(s + 1 + core, 2)
        return (level * 4 + (x ^ e)) * 4 * NB

    ins = []
    for i, (e, s) in enumerate(groups):
        cols = pl.ds(pl.multiple_of(start_of(e, s), 4 * NB), 4 * NB)
        ins.append(pltpu.make_async_copy(a_ref.at[:, cols], a_buf.at[i], in_sem.at[i]))
        ins[-1].start()
    if last:
        col_buf, res_buf, piece_buf, col_sem, res_sem = refs[5:]
        col_in = pltpu.make_async_copy(a_ref.at[:, :NB], col_buf, col_sem)
        col_in.start()
    hi, both = panels(y, p_refs)

    special = y == 1
    if last:
        for e in range(4):
            for s in range(2):
                for d in range(4):

                    @pl.when((x == e) & (core == 1 - s) & (slots[d] == 0))
                    def _():
                        piece_buf[...] = pieces[2 * e + s][d * NB : (d + 1) * NB, :]

        col_in.wait()

        @pl.when(special)
        def _():
            column = col_buf[...] - times_transposed(hi, both, piece_buf[...])
            solved = lax.dot_general(
                column, inv_ref[...], TRANS, precision=HIGH, preferred_element_type=jnp.float32
            )
            res_buf[NB:, :] = solved[NB:]
            keep = jnp.where(row == 1, low_ref[...], solved[:NB])
            res_buf[:NB, :] = jnp.where(row == 0, column[:NB], keep)
            pltpu.make_async_copy(res_buf, out_ref.at[:, :NB], res_sem).start()

    outs = []
    for i, (e, s) in enumerate(groups):
        ref = pieces[2 * e + s] if last else pieces[i]
        prod = times_transposed(hi, both, ref[: 4 * NB, :])
        ins[i].wait()
        for d in range(4):
            cols = pl.ds(pl.multiple_of(slots[d] * NB, NB), NB)
            o_buf[i, :, cols] = a_buf[i, :, cols] - prod[:, d * NB : (d + 1) * NB]
        begin = start_of(e, s)
        for d in range(4):
            cols = pl.ds(pl.multiple_of(begin + d * NB, NB), NB)
            copy = pltpu.make_async_copy(
                o_buf.at[i, :, d * NB : (d + 1) * NB], out_ref.at[:, cols], out_sem.at[i, d]
            )
            write = jnp.logical_not(special & (begin + d * NB == 0)) if last else None
            outs.append((copy, write))
            if write is None:
                copy.start()
            else:
                pl.when(write)(copy.start)
    for copy, write in outs:
        if write is None:
            copy.wait()
        else:
            pl.when(write)(copy.wait)
    if last:

        @pl.when(special)
        def _():
            pltpu.make_async_copy(res_buf, out_ref.at[:, :NB], res_sem).wait()


def vmem():
    return pl.BlockSpec(memory_space=pltpu.VMEM)


def update(hops, matrix, cands, pieces, out=None, factors=()):
    last = len(factors) > 0
    groups = 2 * len(hops)
    hbm = pl.BlockSpec(memory_space=pltpu.HBM)
    args = [matrix, *cands, *pieces, *factors]
    specs = [hbm] + [vmem()] * (len(args) - 1)
    alias = {}
    if out is not None:
        alias = {len(args): 0}
        args.append(out)
        specs.append(hbm)
    scratch = [
        pltpu.VMEM((groups, 2 * NB, 4 * NB), jnp.float32),
        pltpu.VMEM((groups, 2 * NB, 4 * NB), jnp.float32),
        pltpu.SemaphoreType.DMA((groups,)),
        pltpu.SemaphoreType.DMA((groups, 4)),
    ]
    if last:
        scratch += [
            pltpu.VMEM((2 * NB, NB), jnp.float32),
            pltpu.VMEM((2 * NB, NB), jnp.float32),
            pltpu.VMEM((NB, NB), jnp.float32),
            pltpu.SemaphoreType.DMA,
            pltpu.SemaphoreType.DMA,
        ]

    def kernel(*refs):
        update_kernel(hops, last, *refs)

    return pl.pallas_call(
        kernel,
        out_shape=jax.ShapeDtypeStruct(matrix.shape, jnp.float32),
        in_specs=specs,
        out_specs=hbm,
        scratch_shapes=scratch,
        input_output_aliases=alias,
        compiler_params=pltpu.CompilerParams(vmem_limit_bytes=16 * MIB),
        cost_estimate=pl.CostEstimate(
            flops=groups * 2 * NB * NB * 4 * NB * 8,
            bytes_accessed=groups * 2 * NB * 4 * NB * 8,
            transcendentals=0,
        ),
    )(*args)


def on_device(matrix):
    x, z, core, y, row = place()
    tile = jax.ShapeDtypeStruct((NB, NB), jnp.float32)

    panel = matrix[:, :NB]
    panel = jnp.where((jnp.arange(2 * NB) >= NB)[:, None] | (row > 0), panel, 0.0)

    plane = lambda X, Y, Z, C: 2 * (Z % 2) + C
    source = lambda X, Y, Z, C: Y == 0
    got_a = move(panel[:NB], lambda X, Y, Z, C: (X, plane(X, Y, Z, C), Z, 1), source)
    got_b = move(panel[NB:], lambda X, Y, Z, C: (X, plane(X, Y, Z, C), Z, 0), source)
    piece = jnp.where(core == 1, got_a, got_b)

    lower, inverse = pl.pallas_call(
        factor_kernel,
        out_shape=(tile, tile),
        in_specs=[vmem(), vmem()],
        out_specs=(vmem(), vmem()),
        scratch_shapes=[pltpu.VMEM((NB, NB), jnp.float32)],
        compiler_params=pltpu.CompilerParams(vmem_limit_bytes=8 * MIB),
        cost_estimate=pl.CostEstimate(
            flops=10**8, bytes_accessed=3 * NB * NB * 4, transcendentals=0
        ),
    )(panel[:NB], piece)
    other = lambda X, Y, Z, C: (X, Y, Z, 1 - C)
    seed = jnp.where(core == 1, inverse[HALF:], move(inverse[:HALF], other))
    own, piece = lax.optimization_barrier((panel, piece))

    holds = lambda X, Y, Z, C: Z % 2 == Y // 2
    mirrored = move(jnp.concatenate([piece, seed]), lambda X, Y, Z, C: (X, Y, 7 - Z, C), holds)

    rows_a = move(own, lambda X, Y, Z, C: (X, Y ^ 1, Z, C))
    mirrored, rows_a = lax.optimization_barrier((mirrored, rows_a))
    holder = z % 2 == y // 2
    piece = jnp.where(holder, piece, mirrored[:NB])
    seed = jnp.where(z == 7, mirrored[NB:], seed)

    got = move(jnp.concatenate([piece, seed]), lambda X, Y, Z, C: (X, Y, Z ^ 2, C))
    two = jnp.concatenate([piece, got[:NB]])
    seed = jnp.where((z == 2) | (z == 5), got[NB:], seed)
    got = move(jnp.concatenate([two, seed]), lambda X, Y, Z, C: (X, Y, Z ^ 1, C))
    four = jnp.concatenate([two, got[: 2 * NB]])
    seed = jnp.where((z == 0) | (z == 2) | (z == 5) | (z == 7), seed, got[2 * NB :])

    full = jnp.concatenate([four, seed])
    near_a = move(full, lambda X, Y, Z, C: (X ^ 1, Y, Z, C))
    near_b = move(full, lambda X, Y, Z, C: (X ^ 3, Y, Z, C))
    four_o = move(four, other)
    forward = pl.pallas_call(
        forward_kernel,
        out_shape=jax.ShapeDtypeStruct(panel.shape, jnp.float32),
        in_specs=[vmem(), vmem()],
        out_specs=vmem(),
        compiler_params=pltpu.CompilerParams(vmem_limit_bytes=8 * MIB),
        cost_estimate=pl.CostEstimate(
            flops=5 * 10**9, bytes_accessed=6 * NB * NB * 4, transcendentals=0
        ),
    )(panel, rows_a)
    rows_b = move(forward, lambda X, Y, Z, C: (X, Y ^ 3, Z, C))
    near_a, near_b, rows_b = lax.optimization_barrier((near_a, near_b, rows_b))
    cands = [panel, rows_a, rows_b]
    far_a = move(
        jnp.concatenate([near_b[: 2 * NB], near_b[4 * NB :]]),
        lambda X, Y, Z, C: (X ^ 1, Y, Z, C),
    )
    far_b = move(near_a[2 * NB : 4 * NB], lambda X, Y, Z, C: (X ^ 3, Y, Z, C))
    near_a_o, near_b_o = move(near_a[: 4 * NB], other), move(near_b[: 4 * NB], other)
    near = [four, four_o, near_a, near_a_o, near_b, near_b_o]
    out = update((0, 1, 3), matrix, cands, near)
    far_a, far_b, out = lax.optimization_barrier((far_a, far_b, out))
    seed = jnp.where(x == 1, near_a[4 * NB :], seed)
    seed = jnp.where(x == 3, near_b[4 * NB :], seed)
    seed = jnp.where(x == 2, far_a[2 * NB :], seed)
    far = jnp.concatenate([far_a[: 2 * NB], far_b, seed])
    far_o = move(far, other)
    inverse = jnp.where(
        core == 1,
        jnp.concatenate([far_o[4 * NB :], seed]),
        jnp.concatenate([seed, far_o[4 * NB :]]),
    )
    pieces = [four, four_o, near_a, near_a_o, far, far_o, near_b, near_b_o]
    return update((2,), matrix, cands, pieces, out, (lower, inverse))


def solution(mesh):
    return jax.shard_map(
        on_device,
        mesh=mesh,
        in_specs=(P("row", "col"),),
        out_specs=P("row", "col"),
        check_vma=False,
    )
```

```python
import jax
import jax.numpy as jnp
from jax import lax
from jax.experimental import pallas as pl
from jax.experimental.pallas import tpu as pltpu
from jax.sharding import PartitionSpec as P

NB = 128
HALF = NB // 2
NX, NY, NZ, NC = 4, 4, 8, 2
AXES = ("row", "col")
HIGH = lax.Precision.HIGHEST
TRANS = (((1,), (1,)), ((), ()))
MIB = 1024 * 1024


def rank(x, y, z, c):
    return ((x * NZ + z) * NC + c) * NY + y


def move(block, to, where=lambda x, y, z, c: True):
    pairs = [
        (rank(x, y, z, c), rank(*to(x, y, z, c)))
        for x in range(NX)
        for z in range(NZ)
        for c in range(NC)
        for y in range(NY)
        if where(x, y, z, c)
    ]
    return lax.ppermute(block, AXES, pairs)


def split(v):
    hi = v.astype(jnp.bfloat16)
    lo = (v - hi.astype(jnp.float32)).astype(jnp.bfloat16)
    return hi, lo


def times_transposed(left_hi, left_both, right):
    hi, lo = split(right)
    both = lax.dot_general(
        left_both, jnp.concatenate([hi, hi], axis=1), TRANS, preferred_element_type=jnp.float32
    )
    return both + lax.dot_general(left_hi, lo, TRANS, preferred_element_type=jnp.float32)


def place():
    row = lax.axis_index("row")
    return row // (NZ * NC), row // NC % NZ, row % NC, lax.axis_index("col"), row


def factor_kernel(a_ref, p_ref, low_ref, inv_ref, u_ref):
    x, z, core, y, row = place()
    here = (row == 1) & (y == 1)

    @pl.when(here)
    def _():
        factor(a_ref, p_ref, low_ref, inv_ref, u_ref)

    @pl.when(jnp.logical_not(here))
    def _():
        low_ref[...] = jnp.zeros((NB, NB), jnp.float32)
        inv_ref[...] = jnp.zeros((NB, NB), jnp.float32)


def factor(a_ref, p_ref, low_ref, inv_ref, u_ref):
    p = p_ref[...]
    u_ref[...] = a_ref[...] - lax.dot_general(
        p, p, TRANS, precision=HIGH, preferred_element_type=jnp.float32
    )
    n = NB // 8
    lane = lax.broadcasted_iota(jnp.int32, (8, NB), 1)
    sub = lax.broadcasted_iota(jnp.int32, (8, NB), 0)
    s = [u_ref[8 * i : 8 * i + 8, :] for i in range(n)]
    t = [(lane == sub + 8 * i).astype(jnp.float32) for i in range(n)]

    def spread(v, k):
        return jnp.broadcast_to(v[k : k + 1, :], (8, NB))

    for b in range(n):
        cols = [
            [jnp.broadcast_to(s[i][:, 8 * b + k : 8 * b + k + 1], (8, NB)) for i in range(b, n)]
            for k in range(8)
        ]
        factors = []
        for k in range(8):
            inv = 1.0 / spread(cols[k][0], k)
            f = [c * inv for c in cols[k]]
            f[0] = jnp.where(sub > k, f[0], 0.0)
            factors.append(f)
            for m in range(k + 1, 8):
                e = spread(cols[m][0], k)
                cols[m] = [c - g * e for c, g in zip(cols[m], f)]
            r, q = spread(s[b], k), spread(t[b], k)
            s[b] = s[b] - f[0] * r
            t[b] = t[b] - f[0] * q
        for k in range(8):
            r, q = spread(s[b], k), spread(t[b], k)
            for i in range(1, n - b):
                s[b + i] = s[b + i] - factors[k][i] * r
                t[b + i] = t[b + i] - factors[k][i] * q
    upper = []
    for i in range(n):
        diag = jnp.sum(jnp.where(lane == sub + 8 * i, s[i], 0.0), axis=1, keepdims=True)
        scale = 1.0 / jnp.sqrt(diag)
        upper.append(jnp.where(lane >= sub + 8 * i, s[i] * scale, 0.0))
        inv_ref[8 * i : 8 * i + 8, :] = t[i] * scale
    low_ref[...] = jnp.concatenate(upper, axis=0).T


def forward_kernel(panel_ref, rows_ref, out_ref):
    x, z, core, y, row = place()
    out_ref[...] = jnp.where(y == 1, rows_ref[...], panel_ref[...])


def rows_kernel(panel_ref, rows_a_ref, rows_b_ref, out_ref):
    x, z, core, y, row = place()
    later = jnp.where(y == 1, rows_a_ref[...], rows_b_ref[...])
    out_ref[...] = jnp.where(y == 0, panel_ref[...], later)


def stage_kernel(a_ref, out_ref, sem):
    copy = pltpu.make_async_copy(a_ref, out_ref, sem)
    copy.start()
    copy.wait()


def panels(p_ref):
    hi, lo = split(p_ref[...])
    return hi, jnp.concatenate([hi, lo], axis=1)


def update_kernel(hops, last, aliased, a_ref, *refs):
    p_ref, refs = refs[0], refs[1:]
    count = 8 if last else 2 * len(hops)
    pieces, refs = refs[:count], refs[count:]
    if last:
        low_ref, inv_ref, refs = refs[0], refs[1], refs[2:]
    if aliased:
        refs = refs[1:]
    out_ref, a_buf, o_buf, in_sem, out_sem = refs[:5]
    x, z, core, y, row = place()
    even = z % 2 == y // 2
    slots = [jnp.where(even ^ (d % 2 == 1), z ^ d, 7 - (z ^ d)) // 2 for d in (0, 2, 1, 3)]
    groups = [(e, s) for e in hops for s in range(2)]

    def start_of(e, s):
        level = lax.rem(s + 1 + core, 2)
        return (level * 4 + (x ^ e)) * 4 * NB

    ins = []
    for i, (e, s) in enumerate(groups):
        cols = pl.ds(pl.multiple_of(start_of(e, s), 4 * NB), 4 * NB)
        ins.append(pltpu.make_async_copy(a_ref.at[:, cols], a_buf.at[i], in_sem.at[i]))
        ins[-1].start()
    if last:
        col_buf, res_buf, piece_buf, col_sem, res_sem = refs[5:]
        col_in = pltpu.make_async_copy(a_ref.at[:, :NB], col_buf, col_sem)
        col_in.start()
    hi, both = panels(p_ref)

    special = y == 1
    if last:
        for e in range(4):
            for s in range(2):
                for d in range(4):

                    @pl.when((x == e) & (core == 1 - s) & (slots[d] == 0))
                    def _():
                        piece_buf[...] = pieces[2 * e + s][d * NB : (d + 1) * NB, :]

        col_in.wait()

        @pl.when(special)
        def _():
            column = col_buf[...] - times_transposed(hi, both, piece_buf[...])
            solved = lax.dot_general(
                column, inv_ref[...], TRANS, precision=HIGH, preferred_element_type=jnp.float32
            )
            res_buf[NB:, :] = solved[NB:]
            keep = jnp.where(row == 1, low_ref[...], solved[:NB])
            res_buf[:NB, :] = jnp.where(row == 0, column[:NB], keep)
            pltpu.make_async_copy(res_buf, out_ref.at[:, :NB], res_sem).start()

    outs = []
    for i, (e, s) in enumerate(groups):
        ref = pieces[2 * e + s] if last else pieces[i]
        prod = times_transposed(hi, both, ref[: 4 * NB, :])
        ins[i].wait()
        for d in range(4):
            cols = pl.ds(pl.multiple_of(slots[d] * NB, NB), NB)
            o_buf[i, :, cols] = a_buf[i, :, cols] - prod[:, d * NB : (d + 1) * NB]
        begin = start_of(e, s)
        for d in range(4):
            cols = pl.ds(pl.multiple_of(begin + d * NB, NB), NB)
            copy = pltpu.make_async_copy(
                o_buf.at[i, :, d * NB : (d + 1) * NB], out_ref.at[:, cols], out_sem.at[i, d]
            )
            write = jnp.logical_not(special & (begin + d * NB == 0)) if last else None
            outs.append((copy, write))
            if write is None:
                copy.start()
            else:
                pl.when(write)(copy.start)
    for copy, write in outs:
        if write is None:
            copy.wait()
        else:
            pl.when(write)(copy.wait)
    if last:

        @pl.when(special)
        def _():
            pltpu.make_async_copy(res_buf, out_ref.at[:, :NB], res_sem).wait()


def vmem():
    return pl.BlockSpec(memory_space=pltpu.VMEM)


def update(hops, matrix, rows, pieces, out=None, factors=()):
    last = len(factors) > 0
    groups = 2 * len(hops)
    hbm = pl.BlockSpec(memory_space=pltpu.HBM)
    free = pl.BlockSpec(memory_space=pl.ANY)
    args = [matrix, rows, *pieces, *factors]
    specs = [free] + [vmem()] * (len(args) - 1)
    alias = {}
    if out is not None:
        alias = {len(args): 0}
        args.append(out)
        specs.append(hbm)
    scratch = [
        pltpu.VMEM((groups, 2 * NB, 4 * NB), jnp.float32),
        pltpu.VMEM((groups, 2 * NB, 4 * NB), jnp.float32),
        pltpu.SemaphoreType.DMA((groups,)),
        pltpu.SemaphoreType.DMA((groups, 4)),
    ]
    if last:
        scratch += [
            pltpu.VMEM((2 * NB, NB), jnp.float32),
            pltpu.VMEM((2 * NB, NB), jnp.float32),
            pltpu.VMEM((NB, NB), jnp.float32),
            pltpu.SemaphoreType.DMA,
            pltpu.SemaphoreType.DMA,
        ]

    def kernel(*refs):
        update_kernel(hops, last, out is not None, *refs)

    return pl.pallas_call(
        kernel,
        out_shape=jax.ShapeDtypeStruct(matrix.shape, jnp.float32),
        in_specs=specs,
        out_specs=hbm,
        scratch_shapes=scratch,
        input_output_aliases=alias,
        compiler_params=pltpu.CompilerParams(vmem_limit_bytes=16 * MIB),
        cost_estimate=pl.CostEstimate(
            flops=groups * 2 * NB * NB * 4 * NB * 8,
            bytes_accessed=groups * 2 * NB * 4 * NB * 8,
            transcendentals=0,
        ),
    )(*args)


def on_device(matrix):
    x, z, core, y, row = place()
    tile = jax.ShapeDtypeStruct((NB, NB), jnp.float32)

    panel = matrix[:, :NB]
    panel = jnp.where((jnp.arange(2 * NB) >= NB)[:, None] | (row > 0), panel, 0.0)

    plane = lambda X, Y, Z, C: 2 * (Z % 2) + C
    source = lambda X, Y, Z, C: Y == 0
    got_a = move(panel[:NB], lambda X, Y, Z, C: (X, plane(X, Y, Z, C), Z, 1), source)
    got_b = move(panel[NB:], lambda X, Y, Z, C: (X, plane(X, Y, Z, C), Z, 0), source)
    piece = jnp.where(core == 1, got_a, got_b)

    lower, inverse = pl.pallas_call(
        factor_kernel,
        out_shape=(tile, tile),
        in_specs=[vmem(), vmem()],
        out_specs=(vmem(), vmem()),
        scratch_shapes=[pltpu.VMEM((NB, NB), jnp.float32)],
        compiler_params=pltpu.CompilerParams(vmem_limit_bytes=8 * MIB),
        cost_estimate=pl.CostEstimate(
            flops=10**8, bytes_accessed=3 * NB * NB * 4, transcendentals=0
        ),
    )(panel[:NB], piece)
    other = lambda X, Y, Z, C: (X, Y, Z, 1 - C)
    seed = jnp.where(core == 1, inverse[HALF:], move(inverse[:HALF], other))
    own, piece = lax.optimization_barrier((panel, piece))

    holds = lambda X, Y, Z, C: Z % 2 == Y // 2
    mirrored = move(jnp.concatenate([piece, seed]), lambda X, Y, Z, C: (X, Y, 7 - Z, C), holds)

    rows_a = move(own, lambda X, Y, Z, C: (X, Y ^ 1, Z, C))
    mirrored, rows_a = lax.optimization_barrier((mirrored, rows_a))
    holder = z % 2 == y // 2
    piece = jnp.where(holder, piece, mirrored[:NB])
    seed = jnp.where(z == 7, mirrored[NB:], seed)

    got = move(jnp.concatenate([piece, seed]), lambda X, Y, Z, C: (X, Y, Z ^ 2, C))
    two = jnp.concatenate([piece, got[:NB]])
    seed = jnp.where((z == 2) | (z == 5), got[NB:], seed)
    got = move(jnp.concatenate([two, seed]), lambda X, Y, Z, C: (X, Y, Z ^ 1, C))
    four = jnp.concatenate([two, got[: 2 * NB]])
    seed = jnp.where((z == 0) | (z == 2) | (z == 5) | (z == 7), seed, got[2 * NB :])

    full = jnp.concatenate([four, seed])
    near_a = move(full, lambda X, Y, Z, C: (X ^ 1, Y, Z, C))
    near_b = move(full, lambda X, Y, Z, C: (X ^ 3, Y, Z, C))
    four_o = move(four, other)
    forward = pl.pallas_call(
        forward_kernel,
        out_shape=jax.ShapeDtypeStruct(panel.shape, jnp.float32),
        in_specs=[vmem(), vmem()],
        out_specs=vmem(),
        compiler_params=pltpu.CompilerParams(vmem_limit_bytes=8 * MIB),
        cost_estimate=pl.CostEstimate(
            flops=5 * 10**9, bytes_accessed=6 * NB * NB * 4, transcendentals=0
        ),
    )(panel, rows_a)
    rows_b = move(forward, lambda X, Y, Z, C: (X, Y ^ 3, Z, C))
    staged = pl.pallas_call(
        stage_kernel,
        out_shape=jax.ShapeDtypeStruct(matrix.shape, jnp.float32),
        in_specs=[pl.BlockSpec(memory_space=pl.ANY)],
        out_specs=pl.BlockSpec(memory_space=pl.ANY),
        scratch_shapes=[pltpu.SemaphoreType.DMA],
        compiler_params=pltpu.CompilerParams(vmem_limit_bytes=8 * MIB),
        cost_estimate=pl.CostEstimate(
            flops=5 * 10**9, bytes_accessed=8 * MIB, transcendentals=0
        ),
    )(matrix)
    near_a, near_b, rows_b, four_o, staged = lax.optimization_barrier(
        (near_a, near_b, rows_b, four_o, staged)
    )
    rows = pl.pallas_call(
        rows_kernel,
        out_shape=jax.ShapeDtypeStruct(panel.shape, jnp.float32),
        in_specs=[vmem(), vmem(), vmem()],
        out_specs=vmem(),
        compiler_params=pltpu.CompilerParams(vmem_limit_bytes=8 * MIB),
        cost_estimate=pl.CostEstimate(
            flops=5 * 10**9, bytes_accessed=8 * NB * NB * 4, transcendentals=0
        ),
    )(panel, rows_a, rows_b)
    far_a = move(
        jnp.concatenate([near_b[: 2 * NB], near_b[4 * NB :]]),
        lambda X, Y, Z, C: (X ^ 1, Y, Z, C),
    )
    far_b = move(near_a[2 * NB : 4 * NB], lambda X, Y, Z, C: (X ^ 3, Y, Z, C))
    near_a_o, near_b_o = move(near_a[: 4 * NB], other), move(near_b[: 4 * NB], other)
    out = update((1, 3), staged, rows, [near_a, near_a_o, near_b, near_b_o])
    far_a, far_b, out = lax.optimization_barrier((far_a, far_b, out))
    seed = jnp.where(x == 1, near_a[4 * NB :], seed)
    seed = jnp.where(x == 3, near_b[4 * NB :], seed)
    seed = jnp.where(x == 2, far_a[2 * NB :], seed)
    far = jnp.concatenate([far_a[: 2 * NB], far_b, seed])
    far_o = move(far, other)
    out = update((0,), staged, rows, [four, four_o], out)
    inverse = jnp.where(
        core == 1,
        jnp.concatenate([far_o[4 * NB :], seed]),
        jnp.concatenate([seed, far_o[4 * NB :]]),
    )
    pieces = [four, four_o, near_a, near_a_o, far, far_o, near_b, near_b_o]
    return update((2,), staged, rows, pieces, out, (lower, inverse))


def solution(mesh):
    return jax.shard_map(
        on_device,
        mesh=mesh,
        in_specs=(P("row", "col"),),
        out_specs=P("row", "col"),
        check_vma=False,
    )
```

```python
import jax
import jax.numpy as jnp
from jax import lax
from jax.experimental import pallas as pl
from jax.experimental.pallas import tpu as pltpu
from jax.sharding import PartitionSpec as P

NB = 128
HALF = NB // 2
NX, NY, NZ, NC = 4, 4, 8, 2
AXES = ("row", "col")
HIGH = lax.Precision.HIGHEST
TRANS = (((1,), (1,)), ((), ()))
MIB = 1024 * 1024


def rank(x, y, z, c):
    return ((x * NZ + z) * NC + c) * NY + y


def move(block, to, where=lambda x, y, z, c: True):
    pairs = [
        (rank(x, y, z, c), rank(*to(x, y, z, c)))
        for x in range(NX)
        for z in range(NZ)
        for c in range(NC)
        for y in range(NY)
        if where(x, y, z, c)
    ]
    return lax.ppermute(block, AXES, pairs)


def split(v):
    hi = v.astype(jnp.bfloat16)
    lo = (v - hi.astype(jnp.float32)).astype(jnp.bfloat16)
    return hi, lo


def times_transposed(left_hi, left_both, right):
    hi, lo = split(right)
    both = lax.dot_general(
        left_both, jnp.concatenate([hi, hi], axis=1), TRANS, preferred_element_type=jnp.float32
    )
    return both + lax.dot_general(left_hi, lo, TRANS, preferred_element_type=jnp.float32)


def place():
    row = lax.axis_index("row")
    return row // (NZ * NC), row // NC % NZ, row % NC, lax.axis_index("col"), row


def factor_kernel(a_ref, p_ref, low_ref, inv_ref, u_ref):
    x, z, core, y, row = place()
    here = (row == 1) & (y == 1)

    @pl.when(here)
    def _():
        factor(a_ref, p_ref, low_ref, inv_ref, u_ref)

    @pl.when(jnp.logical_not(here))
    def _():
        low_ref[...] = jnp.zeros((NB, NB), jnp.float32)
        inv_ref[...] = jnp.zeros((NB, NB), jnp.float32)


def factor(a_ref, p_ref, low_ref, inv_ref, u_ref):
    p = p_ref[...]
    u_ref[...] = a_ref[...] - lax.dot_general(
        p, p, TRANS, precision=HIGH, preferred_element_type=jnp.float32
    )
    n = NB // 8
    lane = lax.broadcasted_iota(jnp.int32, (8, NB), 1)
    sub = lax.broadcasted_iota(jnp.int32, (8, NB), 0)
    s = [u_ref[8 * i : 8 * i + 8, :] for i in range(n)]
    t = [(lane == sub + 8 * i).astype(jnp.float32) for i in range(n)]

    def spread(v, k):
        return jnp.broadcast_to(v[k : k + 1, :], (8, NB))

    for b in range(n):
        cols = [
            [jnp.broadcast_to(s[i][:, 8 * b + k : 8 * b + k + 1], (8, NB)) for i in range(b, n)]
            for k in range(8)
        ]
        factors = []
        for k in range(8):
            inv = 1.0 / spread(cols[k][0], k)
            f = [c * inv for c in cols[k]]
            f[0] = jnp.where(sub > k, f[0], 0.0)
            factors.append(f)
            for m in range(k + 1, 8):
                e = spread(cols[m][0], k)
                cols[m] = [c - g * e for c, g in zip(cols[m], f)]
            r, q = spread(s[b], k), spread(t[b], k)
            s[b] = s[b] - f[0] * r
            t[b] = t[b] - f[0] * q
        for k in range(8):
            r, q = spread(s[b], k), spread(t[b], k)
            for i in range(1, n - b):
                s[b + i] = s[b + i] - factors[k][i] * r
                t[b + i] = t[b + i] - factors[k][i] * q
    upper = []
    for i in range(n):
        diag = jnp.sum(jnp.where(lane == sub + 8 * i, s[i], 0.0), axis=1, keepdims=True)
        scale = 1.0 / jnp.sqrt(diag)
        upper.append(jnp.where(lane >= sub + 8 * i, s[i] * scale, 0.0))
        inv_ref[8 * i : 8 * i + 8, :] = t[i] * scale
    low_ref[...] = jnp.concatenate(upper, axis=0).T


def forward_kernel(panel_ref, rows_ref, out_ref):
    x, z, core, y, row = place()
    out_ref[...] = jnp.where(y == 1, rows_ref[...], panel_ref[...])


def rows_kernel(panel_ref, rows_a_ref, rows_b_ref, out_ref):
    x, z, core, y, row = place()
    later = jnp.where(y == 1, rows_a_ref[...], rows_b_ref[...])
    out_ref[...] = jnp.where(y == 0, panel_ref[...], later)


def stage_kernel(a_ref, out_ref, sem):
    copy = pltpu.make_async_copy(a_ref, out_ref, sem)
    copy.start()
    copy.wait()


def panels(p_ref):
    hi, lo = split(p_ref[...])
    return hi, jnp.concatenate([hi, lo], axis=1)


def update_kernel(hops, last, aliased, a_ref, *refs):
    p_ref, refs = refs[0], refs[1:]
    count = 8 if last else 2 * len(hops)
    pieces, refs = refs[:count], refs[count:]
    if last:
        low_ref, inv_ref, refs = refs[0], refs[1], refs[2:]
    if aliased:
        refs = refs[1:]
    out_ref, a_buf, o_buf, in_sem, out_sem = refs[:5]
    x, z, core, y, row = place()
    even = z % 2 == y // 2
    slots = [jnp.where(even ^ (d % 2 == 1), z ^ d, 7 - (z ^ d)) // 2 for d in (0, 2, 1, 3)]
    groups = [(e, s) for e in hops for s in range(2)]

    def start_of(e, s):
        level = lax.rem(s + 1 + core, 2)
        return (level * 4 + (x ^ e)) * 4 * NB

    ins = []
    for i, (e, s) in enumerate(groups):
        cols = pl.ds(pl.multiple_of(start_of(e, s), 4 * NB), 4 * NB)
        ins.append(pltpu.make_async_copy(a_ref.at[:, cols], a_buf.at[i], in_sem.at[i]))
        ins[-1].start()
    if last:
        col_buf, res_buf, piece_buf, col_sem, res_sem = refs[5:]
        col_in = pltpu.make_async_copy(a_ref.at[:, :NB], col_buf, col_sem)
        col_in.start()
    hi, both = panels(p_ref)

    special = y == 1
    if last:
        for e in range(4):
            for s in range(2):
                for d in range(4):

                    @pl.when((x == e) & (core == 1 - s) & (slots[d] == 0))
                    def _():
                        piece_buf[...] = pieces[2 * e + s][d * NB : (d + 1) * NB, :]

        col_in.wait()

        @pl.when(special)
        def _():
            column = col_buf[...] - times_transposed(hi, both, piece_buf[...])
            solved = lax.dot_general(
                column, inv_ref[...], TRANS, precision=HIGH, preferred_element_type=jnp.float32
            )
            res_buf[NB:, :] = solved[NB:]
            keep = jnp.where(row == 1, low_ref[...], solved[:NB])
            res_buf[:NB, :] = jnp.where(row == 0, column[:NB], keep)
            pltpu.make_async_copy(res_buf, out_ref.at[:, :NB], res_sem).start()

    outs = []
    for i, (e, s) in enumerate(groups):
        ref = pieces[2 * e + s] if last else pieces[i]
        prod = times_transposed(hi, both, ref[: 4 * NB, :])
        ins[i].wait()
        for d in range(4):
            cols = pl.ds(pl.multiple_of(slots[d] * NB, NB), NB)
            o_buf[i, :, cols] = a_buf[i, :, cols] - prod[:, d * NB : (d + 1) * NB]
        begin = start_of(e, s)
        for d in range(4):
            cols = pl.ds(pl.multiple_of(begin + d * NB, NB), NB)
            copy = pltpu.make_async_copy(
                o_buf.at[i, :, d * NB : (d + 1) * NB], out_ref.at[:, cols], out_sem.at[i, d]
            )
            write = jnp.logical_not(special & (begin + d * NB == 0)) if last else None
            outs.append((copy, write))
            if write is None:
                copy.start()
            else:
                pl.when(write)(copy.start)
    for copy, write in outs:
        if write is None:
            copy.wait()
        else:
            pl.when(write)(copy.wait)
    if last:

        @pl.when(special)
        def _():
            pltpu.make_async_copy(res_buf, out_ref.at[:, :NB], res_sem).wait()


def vmem():
    return pl.BlockSpec(memory_space=pltpu.VMEM)


def update(hops, matrix, rows, pieces, out=None, factors=()):
    last = len(factors) > 0
    groups = 2 * len(hops)
    hbm = pl.BlockSpec(memory_space=pltpu.HBM)
    free = pl.BlockSpec(memory_space=pl.ANY)
    args = [matrix, rows, *pieces, *factors]
    specs = [free] + [vmem()] * (len(args) - 1)
    alias = {}
    if out is not None:
        alias = {len(args): 0}
        args.append(out)
        specs.append(hbm)
    scratch = [
        pltpu.VMEM((groups, 2 * NB, 4 * NB), jnp.float32),
        pltpu.VMEM((groups, 2 * NB, 4 * NB), jnp.float32),
        pltpu.SemaphoreType.DMA((groups,)),
        pltpu.SemaphoreType.DMA((groups, 4)),
    ]
    if last:
        scratch += [
            pltpu.VMEM((2 * NB, NB), jnp.float32),
            pltpu.VMEM((2 * NB, NB), jnp.float32),
            pltpu.VMEM((NB, NB), jnp.float32),
            pltpu.SemaphoreType.DMA,
            pltpu.SemaphoreType.DMA,
        ]

    def kernel(*refs):
        update_kernel(hops, last, out is not None, *refs)

    return pl.pallas_call(
        kernel,
        out_shape=jax.ShapeDtypeStruct(matrix.shape, jnp.float32),
        in_specs=specs,
        out_specs=hbm,
        scratch_shapes=scratch,
        input_output_aliases=alias,
        compiler_params=pltpu.CompilerParams(vmem_limit_bytes=16 * MIB),
        cost_estimate=pl.CostEstimate(
            flops=groups * 2 * NB * NB * 4 * NB * 8,
            bytes_accessed=groups * 2 * NB * 4 * NB * 8,
            transcendentals=0,
        ),
    )(*args)


def on_device(matrix):
    x, z, core, y, row = place()
    tile = jax.ShapeDtypeStruct((NB, NB), jnp.float32)

    panel = matrix[:, :NB]
    panel = jnp.where((jnp.arange(2 * NB) >= NB)[:, None] | (row > 0), panel, 0.0)

    plane = lambda X, Y, Z, C: 2 * (Z % 2) + C
    source = lambda X, Y, Z, C: Y == 0
    got_a = move(panel[:NB], lambda X, Y, Z, C: (X, plane(X, Y, Z, C), Z, 1), source)
    got_b = move(panel[NB:], lambda X, Y, Z, C: (X, plane(X, Y, Z, C), Z, 0), source)
    piece = jnp.where(core == 1, got_a, got_b)

    lower, inverse = pl.pallas_call(
        factor_kernel,
        out_shape=(tile, tile),
        in_specs=[vmem(), vmem()],
        out_specs=(vmem(), vmem()),
        scratch_shapes=[pltpu.VMEM((NB, NB), jnp.float32)],
        compiler_params=pltpu.CompilerParams(vmem_limit_bytes=8 * MIB),
        cost_estimate=pl.CostEstimate(
            flops=10**8, bytes_accessed=3 * NB * NB * 4, transcendentals=0
        ),
    )(panel[:NB], piece)
    other = lambda X, Y, Z, C: (X, Y, Z, 1 - C)
    seed = jnp.where(core == 1, inverse[HALF:], move(inverse[:HALF], other))
    own, piece = lax.optimization_barrier((panel, piece))

    holds = lambda X, Y, Z, C: Z % 2 == Y // 2
    mirrored = move(jnp.concatenate([piece, seed]), lambda X, Y, Z, C: (X, Y, 7 - Z, C), holds)

    rows_a = move(own, lambda X, Y, Z, C: (X, Y ^ 1, Z, C))
    mirrored, rows_a = lax.optimization_barrier((mirrored, rows_a))
    holder = z % 2 == y // 2
    piece = jnp.where(holder, piece, mirrored[:NB])
    seed = jnp.where(z == 7, mirrored[NB:], seed)

    got = move(jnp.concatenate([piece, seed]), lambda X, Y, Z, C: (X, Y, Z ^ 2, C))
    two = jnp.concatenate([piece, got[:NB]])
    seed = jnp.where((z == 2) | (z == 5), got[NB:], seed)
    got = move(jnp.concatenate([two, seed]), lambda X, Y, Z, C: (X, Y, Z ^ 1, C))
    four = jnp.concatenate([two, got[: 2 * NB]])
    seed = jnp.where((z == 0) | (z == 2) | (z == 5) | (z == 7), seed, got[2 * NB :])

    full = jnp.concatenate([four, seed])
    near_a = move(full, lambda X, Y, Z, C: (X ^ 1, Y, Z, C))
    near_b = move(full, lambda X, Y, Z, C: (X ^ 3, Y, Z, C))
    four_o = move(four, other)
    forward = pl.pallas_call(
        forward_kernel,
        out_shape=jax.ShapeDtypeStruct(panel.shape, jnp.float32),
        in_specs=[vmem(), vmem()],
        out_specs=vmem(),
        compiler_params=pltpu.CompilerParams(vmem_limit_bytes=8 * MIB),
        cost_estimate=pl.CostEstimate(
            flops=5 * 10**9, bytes_accessed=6 * NB * NB * 4, transcendentals=0
        ),
    )(panel, rows_a)
    rows_b = move(forward, lambda X, Y, Z, C: (X, Y ^ 3, Z, C))
    staged = pl.pallas_call(
        stage_kernel,
        out_shape=jax.ShapeDtypeStruct(matrix.shape, jnp.float32),
        in_specs=[pl.BlockSpec(memory_space=pl.ANY)],
        out_specs=pl.BlockSpec(memory_space=pl.ANY),
        scratch_shapes=[pltpu.SemaphoreType.DMA],
        compiler_params=pltpu.CompilerParams(vmem_limit_bytes=8 * MIB),
        cost_estimate=pl.CostEstimate(
            flops=5 * 10**9, bytes_accessed=8 * MIB, transcendentals=0
        ),
    )(matrix)
    near_a, near_b, rows_b, four_o, staged = lax.optimization_barrier(
        (near_a, near_b, rows_b, four_o, staged)
    )
    rows = pl.pallas_call(
        rows_kernel,
        out_shape=jax.ShapeDtypeStruct(panel.shape, jnp.float32),
        in_specs=[vmem(), vmem(), vmem()],
        out_specs=vmem(),
        compiler_params=pltpu.CompilerParams(vmem_limit_bytes=8 * MIB),
        cost_estimate=pl.CostEstimate(
            flops=5 * 10**9, bytes_accessed=8 * NB * NB * 4, transcendentals=0
        ),
    )(panel, rows_a, rows_b)
    far_a = move(
        jnp.concatenate([near_b[: 2 * NB], near_b[4 * NB :]]),
        lambda X, Y, Z, C: (X ^ 1, Y, Z, C),
    )
    far_b = move(near_a[2 * NB : 4 * NB], lambda X, Y, Z, C: (X ^ 3, Y, Z, C))
    near_o = move(jnp.concatenate([near_a[: 4 * NB], near_b[: 4 * NB]]), other)
    near_a_o, near_b_o = near_o[: 4 * NB], near_o[4 * NB :]
    out = update((1, 3), staged, rows, [near_a, near_a_o, near_b, near_b_o])
    far_a, far_b, out = lax.optimization_barrier((far_a, far_b, out))
    seed = jnp.where(x == 1, near_a[4 * NB :], seed)
    seed = jnp.where(x == 3, near_b[4 * NB :], seed)
    seed = jnp.where(x == 2, far_a[2 * NB :], seed)
    far = jnp.concatenate([far_a[: 2 * NB], far_b, seed])
    far_o = move(far, other)
    out = update((0,), staged, rows, [four, four_o], out)
    inverse = jnp.where(
        core == 1,
        jnp.concatenate([far_o[4 * NB :], seed]),
        jnp.concatenate([seed, far_o[4 * NB :]]),
    )
    pieces = [four, four_o, near_a, near_a_o, far, far_o, near_b, near_b_o]
    return update((2,), staged, rows, pieces, out, (lower, inverse))


def solution(mesh):
    return jax.shard_map(
        on_device,
        mesh=mesh,
        in_specs=(P("row", "col"),),
        out_specs=P("row", "col"),
        check_vma=False,
    )
```
